256 devices in a mesh: prow: 16 (over y, x), pcol: 16 (over z, core).
Axes of the slice: x: 4, y: 4, z: 8, core: 2. Of those that a mesh axis runs over, the one named last changes fastest.
Arguments:
- matrix: float32 [5, 16, 256, 5, 16, 256], P(None, 'prow', None, None, 'pcol')
Outputs:
- factored: float32 [5, 16, 256, 5, 16, 256], P(None, 'prow', None, None, 'pcol')
All inputs are finite; a program needn't handle non-finite values.
Results may differ from the reference program's by a relative error of at most 0.0003.
Values sent between devices are 32-bit elements; how exact they have to be, the bound alone decides.
A program may use at most 128 MiB of HBM per device.

```python
import math
import jax
import jax.numpy as jnp
from jax import lax

NB = 256
KT = 5
CT = 5
N_PROW = 16
N_PCOL = 16


def draw_matrix(key, part):
    key = jax.random.fold_in(key, 7)
    first, second = jax.random.split(key)
    shape = (KT, N_PROW, NB, CT, N_PCOL, NB)
    base = jax.random.uniform(first, shape, jnp.float32, -0.5, 0.5)
    left_shape = (KT, N_PROW, NB, 1, 1, 1)
    right_shape = (1, 1, 1, CT, N_PCOL, NB)
    row_tile = lax.broadcasted_iota(jnp.int32, left_shape, 0) * N_PROW + lax.broadcasted_iota(jnp.int32, left_shape, 1)
    row_index = row_tile * NB + lax.broadcasted_iota(jnp.int32, left_shape, 2)
    col_tile = lax.broadcasted_iota(jnp.int32, right_shape, 3) * N_PCOL + lax.broadcasted_iota(jnp.int32, right_shape, 4)
    col_index = col_tile * NB + lax.broadcasted_iota(jnp.int32, right_shape, 5)
    lifted = jax.random.uniform(second, shape, jnp.float32, 1.1, 2.0) * (0.5 * (NB - 1))
    values = jnp.where(row_index == col_index, lifted, base)
    in_panel = (col_tile == 0) & (row_tile > 0)
    values = jnp.where(in_panel, base * (0.5 * math.sqrt(NB)), values)
    return values


def setup_inputs(seed: int = 0) -> dict:
    streams_of = jax.random.split(jax.random.key(seed), 2)
    return {
        "matrix": draw_matrix(jax.random.fold_in(streams_of[1], 71), 0),
    }


def reference(matrix):
    order = KT * N_PROW * NB
    whole = matrix.reshape(order, order)
    factor = jnp.linalg.cholesky(whole[:NB, :NB])
    panel = lax.linalg.triangular_solve(factor, whole[:, :NB], left_side=False, lower=True, transpose_a=True)
    panel = panel.at[:NB].set(factor)
    tile_count = order // NB
    col_tile = jnp.arange(order, dtype=jnp.int32) // NB

    def one_row(tile):
        block = lax.dynamic_slice_in_dim(whole, tile * NB, NB, 0)
        left = lax.dynamic_slice_in_dim(panel, tile * NB, NB, 0)
        updated = block - jnp.dot(left, panel.T, precision=lax.Precision.HIGHEST)
        kept = jnp.where((col_tile <= tile)[None, :], updated, jnp.zeros_like(updated))
        return kept.at[:, :NB].set(left)
    rows = lax.map(one_row, jnp.arange(tile_count, dtype=jnp.int32))
    return rows.reshape(KT, N_PROW, NB, CT, N_PCOL, NB)
```

```python
import functools

import jax
import jax.numpy as jnp
from jax import lax
from jax.experimental import pallas as pl
from jax.experimental.pallas import tpu as pltpu
from jax.sharding import PartitionSpec as P

MESH = pl.DeviceIdType.MESH
HI = lax.Precision.HIGHEST
NB, PB, MB = 256, 64, 8
T = 5
ROWS = 64
PER = NB // ROWS
SL = 16


def micro(w_ref, r0, pend):
    lane = lax.broadcasted_iota(jnp.int32, (MB, NB), 1)
    sub = lax.broadcasted_iota(jnp.int32, (MB, NB), 0)
    sub1 = lax.broadcasted_iota(jnp.int32, (MB, 128), 0)
    own = (lane >= r0) & (lane < r0 + MB)
    blk = w_ref[r0:r0 + MB, :]
    d = blk[:, r0:r0 + MB]
    rep = {(i, j): jnp.broadcast_to(d[i:i + 1, j:j + 1], (MB, 128)) for i in range(MB) for j in range(i + 1)}
    low, inv = {}, {}
    a = dict(rep)
    rs = []
    for j in range(MB):
        r = lax.rsqrt(a[j, j])
        rs.append(r)
        for i in range(j + 1, MB):
            low[i, j] = a[i, j] * r
        for k in range(j + 1, MB):
            for i in range(k, MB):
                a[i, k] = a[i, k] - low[i, j] * low[k, j]
    for j in range(MB):
        inv[j, j] = rs[j]
        for i in range(j + 1, MB):
            t = low[i, j] * inv[j, j]
            for k in range(j + 1, i):
                t = t + low[i, k] * inv[k, j]
            inv[i, j] = -t * rs[i]
    ainv = {}
    for i in range(MB):
        for j in range(i + 1):
            t = inv[i, i] * inv[i, j]
            for k in range(i + 1, MB):
                t = t + inv[k, i] * inv[k, j]
            ainv[i, j] = ainv[j, i] = t
    aug = []
    for j in range(MB):
        row = jnp.broadcast_to(w_ref[r0 + j:r0 + j + 1, :], (MB, NB))
        aug.append(jnp.where(own, jnp.where(lane == r0 + j, 1.0, 0.0), row))
    def mix(coef, lower):
        out = None
        for j in range(MB):
            col = jnp.zeros((MB, 128), jnp.float32)
            for i in range(j if lower else 0, MB):
                col = jnp.where(sub1 == i, coef[i, j], col)
            term = jnp.concatenate([col, col], axis=1) * aug[j]
            out = term if out is None else out + term
        return out
    z = mix(ainv, False)
    if pend > r0 + MB:
        rows = w_ref[r0 + MB:pend, :]
        n = pend - r0 - MB
        lane_n = lax.broadcasted_iota(jnp.int32, (n, NB), 1)
        acc = jnp.where((lane_n >= r0) & (lane_n < r0 + MB), 0.0, rows)
        for j in range(MB):
            acc = acc - rows[:, r0 + j:r0 + j + 1] * z[j:j + 1, :]
        w_ref[r0 + MB:pend, :] = acc
    w_ref[r0:r0 + MB, :] = mix(inv, True)

def panel(w_ref, kb):
    p0 = kb * PB
    for m in range(PB // MB):
        micro(w_ref, p0 + m * MB, p0 + PB)
    if p0 + PB < NB:
        r = w_ref[p0:p0 + PB, :]
        n = NB - p0 - PB
        lane_r = lax.broadcasted_iota(jnp.int32, (PB, NB), 1)
        sub_r = lax.broadcasted_iota(jnp.int32, (PB, NB), 0) + p0
        solved = jnp.where((lane_r > sub_r) & (lane_r < p0 + PB), 0.0, r)
        rest = w_ref[p0 + PB:NB, :]
        lane_n = lax.broadcasted_iota(jnp.int32, (n, NB), 1)
        rest = jnp.where((lane_n >= p0) & (lane_n < p0 + PB), 0.0, rest)
        up = lax.dot_general(r[:, p0 + PB:NB], solved, (((0,), (0,)), ((), ())), precision=HI, preferred_element_type=jnp.float32)
        w_ref[p0 + PB:NB, :] = rest - up

def inv_rows(w_ref, kb):
    p0 = kb * PB
    x = w_ref[p0:p0 + PB, :]
    lane = lax.broadcasted_iota(jnp.int32, (PB, NB), 1)
    sub = lax.broadcasted_iota(jnp.int32, (PB, NB), 0) + p0
    return jnp.where(lane <= sub, x, 0.0)


def gather_kernel(a_ref, r_ref, c_ref, i_ref, a_v, w_ref, inv_v, load_sem, send_sem, ysend_sem, csend_sem, r_sem, i_sem, s_sem, g_sem):
    p, q = lax.axis_index("prow"), lax.axis_index("pcol")
    x, y, z, c = lax.rem(p, 4), p // 4, q // 2, lax.rem(q, 2)
    source = q == 0
    owner = jnp.logical_and(p == 0, source)
    bar = pltpu.get_barrier_semaphore()

    def greet(row, col):
        pl.semaphore_signal(bar, 1, device_id=(row, col), device_id_type=MESH)

    def remote(ref, send, recv, row, col):
        return pltpu.make_async_remote_copy(src_ref=ref, dst_ref=ref, send_sem=send, recv_sem=recv, device_id=(row, col), device_id_type=MESH)

    def wait(ref, sem):
        pltpu.make_async_copy(ref, ref, sem).wait()

    def r_chunk(n):
        return r_ref.at[n // PER, pl.ds((n % PER) * ROWS, ROWS), :]

    def i_chunk(m):
        return i_ref.at[pl.ds(m * ROWS, ROWS), :]

    @pl.loop(1, 16)
    def _(d):
        greet(lax.rem(p + d, 16), q)

    @pl.when(jnp.logical_not(owner))
    def _():
        greet(q, 0)

    for kid, parents in ((1, (2,)), (2, (0,)), (3, (2,)), (4, (3, 5)), (5, (6,)), (6, (0,)), (7, (6,))):
        @pl.when(jnp.logical_and(c == 0, z == kid))
        def _(parents=parents):
            for parent in parents:
                greet(p, 2 * parent)

    @pl.when(c == 1)
    def _():
        greet(p, q - 1)

    @pl.when(jnp.logical_and(source, y != 0))
    def _():
        greet(x, 0)

    @pl.when(jnp.logical_and(source, jnp.logical_and(y == 0, x != 0)))
    def _():
        greet(0, 0)

    one = lambda cond: jnp.where(cond, 1, 0)
    near = one(c == 0)
    kids = near + 2 * near * (one(z == 0) + one(z == 2) + one(z == 6)) + near * (one(z == 3) + one(z == 5))
    expect = 15 + one(source) * (16 - one(owner)) + kids + 3 * one(jnp.logical_and(source, y == 0)) + 3 * one(owner)

    def greeted():
        pl.semaphore_wait(bar, expect)

    def pass_on(ref, recv, kids):
        for slot, kid in enumerate(kids):
            remote(ref, send_sem.at[slot], recv, p, 2 * kid).start()
        remote(ref, send_sem.at[2], recv, p, q + 1).start()

    def scatter(t):
        @pl.loop(0, 16)
        def _(s):
            part = pl.ds(pl.multiple_of(s * SL, SL), SL)

            @pl.when(jnp.logical_or(s != 0, jnp.logical_not(owner)))
            def _():
                pltpu.make_async_remote_copy(
                    src_ref=r_ref.at[t, part, :], dst_ref=c_ref.at[t, part, :], send_sem=csend_sem.at[0],
                    recv_sem=s_sem.at[t], device_id=(s, p), device_id_type=MESH).start()

            @pl.when(jnp.logical_and(s == 0, owner))
            def _():
                pltpu.make_async_copy(r_ref.at[t, pl.ds(0, SL), :], c_ref.at[t, pl.ds(0, SL), :], s_sem.at[t]).start()

    mine = pl.ds(pl.multiple_of(p * SL, SL), SL)

    def share(t):
        wait(c_ref.at[t, mine, :], s_sem.at[t])

        @pl.loop(1, 16)
        def _(d):
            remote(c_ref.at[t, mine, :], csend_sem.at[1], g_sem.at[t], lax.rem(p + d, 16), q).start()

    def load(t):
        return pltpu.make_async_copy(a_ref.at[t, 0, :, 0, 0, :], r_ref.at[t], load_sem.at[t])

    @pl.when(owner)
    def _():
        first = pltpu.make_async_copy(a_ref.at[0, 0, :, 0, 0, :], a_v, load_sem.at[0])
        first.start()
        for t in range(1, T):
            load(t).start()
        first.wait()
        a = a_v[...]
        w_ref[...] = 0.5 * (a + a.T)
        a_v[...] = w_ref[...]
        kept = pltpu.make_async_copy(a_v, r_ref.at[0], load_sem.at[0])
        kept.start()
        for kb in range(3):
            panel(w_ref, kb)
            inv_v[kb * PB:(kb + 1) * PB, :] = inv_rows(w_ref, kb)
        kept.wait()
        for t in range(1, T):
            load(t).wait()
        greeted()

        def give(m):
            part = pl.ds(m * ROWS, ROWS)
            src = inv_v.at[part, :]
            to = [(1, 0, 0), (2, 0, 1), (3, 0, 2), (4, 0, 3), (8, 0, 4), (12, 0, 5)]
            for row, col, slot in to:
                pltpu.make_async_remote_copy(src_ref=src, dst_ref=i_chunk(m), send_sem=ysend_sem.at[slot], recv_sem=i_sem.at[m], device_id=(row, col), device_id_type=MESH).start()
            for col, slot in ((4, 0), (12, 1), (1, 2)):
                pltpu.make_async_remote_copy(src_ref=src, dst_ref=i_chunk(m), send_sem=send_sem.at[slot], recv_sem=i_sem.at[m], device_id=(0, col), device_id_type=MESH).start()
            pltpu.make_async_copy(src, i_chunk(m), i_sem.at[m]).start()

        for m in range(3):
            give(m)
        for t in range(T):
            for n in range(PER * t, PER * t + PER):
                pass_on(r_chunk(n), r_sem.at[n], (2, 6))
            scatter(t)
        panel(w_ref, 3)
        inv_v[3 * PB:4 * PB, :] = inv_rows(w_ref, 3)
        give(3)
        for t in range(T):
            share(t)
        for m in range(4):
            wait(i_chunk(m), i_sem.at[m])

    @pl.when(jnp.logical_and(source, jnp.logical_not(owner)))
    def _():
        for t in range(T):
            load(t).start()
        for t in range(T):
            load(t).wait()
        greeted()
        for t in range(T):
            for n in range(PER * t, PER * t + PER):
                pass_on(r_chunk(n), r_sem.at[n], (2, 6))
            scatter(t)
        for m in range(4):
            wait(i_chunk(m), i_sem.at[m])

            @pl.when(y == 0)
            def _():
                for k in range(1, 4):
                    remote(i_chunk(m), ysend_sem.at[k - 1], i_sem.at[m], 4 * k + x, 0).start()
            pass_on(i_chunk(m), i_sem.at[m], (2, 6))
        for t in range(T):
            share(t)

    @pl.when(q != 0)
    def _():
        greeted()

    def relay(ref, sem, n):
        wait(ref, sem)

        @pl.when(z == 2)
        def _():
            for slot, kid in enumerate((1, 3)):
                remote(ref, send_sem.at[slot], sem, p, 2 * kid).start()

        @pl.when(z == 6)
        def _():
            for slot, kid in enumerate((5, 7)):
                remote(ref, send_sem.at[slot], sem, p, 2 * kid).start()

        @pl.when(z == (3 if n % 2 == 0 else 5))
        def _():
            remote(ref, send_sem.at[0], sem, p, 8).start()
        remote(ref, send_sem.at[2], sem, p, q + 1).start()

    @pl.when(jnp.logical_and(c == 0, z != 0))
    def _():
        for t in range(T):
            for n in range(PER * t, PER * t + PER):
                relay(r_chunk(n), r_sem.at[n], n)
            share(t)
        for m in range(4):
            relay(i_chunk(m), i_sem.at[m], m)

    @pl.when(c == 1)
    def _():
        for t in range(T):
            share(t)
        for n in range(T * PER):
            wait(r_chunk(n), r_sem.at[n])
        for m in range(4):
            wait(i_chunk(m), i_sem.at[m])

    for t in range(T):
        wait(c_ref.at[t, pl.ds(0, NB - SL), :], g_sem.at[t])
    wait(c_ref.at[:, pl.ds(0, NB - SL), :], csend_sem.at[1])

    @pl.when(owner)
    def _():
        wait(c_ref.at[:, pl.ds(0, NB - SL), :], csend_sem.at[0])

    @pl.when(jnp.logical_and(source, jnp.logical_not(owner)))
    def _():
        wait(c_ref, csend_sem.at[0])

    @pl.when(jnp.logical_and(source, y == 0))
    def _():
        for k in range(3):
            wait(i_ref, ysend_sem.at[k])

    @pl.when(owner)
    def _():
        for k in range(3, 6):
            wait(i_ref, ysend_sem.at[k])

    def sent(slot):
        wait(r_ref, send_sem.at[slot])
        wait(i_ref, send_sem.at[slot])

    @pl.when(c == 0)
    def _():
        sent(2)

    @pl.when(jnp.logical_and(c == 0, jnp.logical_or(z == 0, jnp.logical_or(z == 2, z == 6))))
    def _():
        sent(0)
        sent(1)

    @pl.when(jnp.logical_and(c == 0, jnp.logical_or(z == 3, z == 5)))
    def _():
        wait(r_ref.at[:, pl.ds(0, NB // 2), :], send_sem.at[0])
        wait(i_ref.at[pl.ds(0, NB // 2), :], send_sem.at[0])


def gather(matrix):
    tiles = jax.ShapeDtypeStruct((T, NB, NB), jnp.float32)
    square = jax.ShapeDtypeStruct((NB, NB), jnp.float32)
    dma = pltpu.SemaphoreType.DMA
    return pl.pallas_call(
        gather_kernel,
        out_shape=(tiles, tiles, square),
        in_specs=[pl.BlockSpec(memory_space=pltpu.HBM)],
        out_specs=[pl.BlockSpec(memory_space=pl.ANY)] * 3,
        scratch_shapes=[
            pltpu.VMEM((NB, NB), jnp.float32), pltpu.VMEM((NB, NB), jnp.float32), pltpu.VMEM((NB, NB), jnp.float32),
            dma((T,)), dma((3,)), dma((6,)), dma((2,)), dma((T * PER,)), dma((4,)), dma((T,)), dma((T,)),
        ],
        compiler_params=pltpu.CompilerParams(collective_id=0, has_side_effects=True, vmem_limit_bytes=16 * 2**20),
        name="gather",
    )(matrix)


def split(v):
    high = v.astype(jnp.bfloat16)
    return high, (v - high.astype(jnp.float32)).astype(jnp.bfloat16)


def times(left, right):
    dims = (((1,), (1,)), ((), ()))
    dot = functools.partial(lax.dot_general, dimension_numbers=dims, preferred_element_type=jnp.float32)
    return dot(left[0], right[0]) + (dot(left[0], right[1]) + dot(left[1], right[0]))


PAIRS = [(k, j) for k in range(T) for j in range(k + 1)]


def update_kernel(a_ref, r_ref, c_ref, i_ref, o_ref, a_v, z_v, x_v, rh, rl, ch, cl, load_sem, store_sem, zero_sem):
    p, q = lax.axis_index("prow"), lax.axis_index("pcol")

    def load(n):
        k, j = PAIRS[n]
        return pltpu.make_async_copy(a_ref.at[k, 0, :, j, 0, :], a_v.at[n], load_sem.at[n])

    def store(n):
        k, j = PAIRS[n]
        return pltpu.make_async_copy(a_v.at[n], o_ref.at[k, 0, :, j, 0, :], store_sem.at[n])

    for n in range(len(PAIRS)):
        load(n).start()
    z_v[...] = jnp.zeros_like(z_v)
    blank = [pltpu.make_async_copy(z_v, o_ref.at[k, 0, :, j, 0, :], zero_sem) for k in range(T) for j in range(k + 1, T)]
    for copy in blank:
        copy.start()
    inv = split(i_ref[...])
    for k in range(T):
        v = times(split(r_ref[k]), inv)
        x_v[k] = v
        rh[k], rl[k] = split(v)
        ch[k], cl[k] = split(times(split(c_ref[k]), inv))

    @pl.when(jnp.logical_and(p == 0, q == 0))
    def _():
        row = lax.broadcasted_iota(jnp.int32, (NB, NB), 0)
        col = lax.broadcasted_iota(jnp.int32, (NB, NB), 1)
        x_v[0] = jnp.where(col <= row, x_v[0], 0.0)

    for n, (k, j) in enumerate(PAIRS):
        load(n).wait()
        v = a_v[n] - times((rh[k], rl[k]), (ch[j], cl[j]))
        if k == j:
            v = jnp.where(p >= q, v, 0.0)
        if j == 0:
            v = jnp.where(q == 0, x_v[k], v)
        a_v[n] = v
        store(n).start()
    for copy in blank:
        copy.wait()
    for n in range(len(PAIRS)):
        store(n).wait()


def update(matrix, r, c, i):
    vmem = pl.BlockSpec(memory_space=pltpu.VMEM)
    half = pltpu.VMEM((T, NB, NB), jnp.bfloat16)
    dma = pltpu.SemaphoreType.DMA
    return pl.pallas_call(
        update_kernel,
        out_shape=jax.ShapeDtypeStruct(matrix.shape, jnp.float32),
        in_specs=[pl.BlockSpec(memory_space=pl.ANY), vmem, vmem, vmem],
        out_specs=pl.BlockSpec(memory_space=pl.ANY),
        scratch_shapes=[
            pltpu.VMEM((len(PAIRS), NB, NB), jnp.float32), pltpu.VMEM((NB, NB), jnp.float32), pltpu.VMEM((T, NB, NB), jnp.float32),
            half, half, half, half, dma((len(PAIRS),)), dma((len(PAIRS),)), dma,
        ],
        compiler_params=pltpu.CompilerParams(vmem_limit_bytes=32 * 2**20),
        name="update",
    )(matrix, r, c, i)


def per_device(matrix):
    r, c, i = gather(matrix)
    return update(matrix, r, c, i)


def solution(mesh):
    spec = P(None, "prow", None, None, "pcol", None)
    return jax.shard_map(per_device, mesh=mesh, in_specs=(spec,), out_specs=spec, check_vma=False)
```

```python
import functools

import jax
import jax.numpy as jnp
from jax import lax
from jax.experimental import pallas as pl
from jax.experimental.pallas import tpu as pltpu
from jax.sharding import PartitionSpec as P

MESH = pl.DeviceIdType.MESH
HI = lax.Precision.HIGHEST
NB, PB, MB = 256, 64, 8
T = 5
ROWS = 64
PER = NB // ROWS
SL = 16


def micro(w_ref, r0, pend):
    lane = lax.broadcasted_iota(jnp.int32, (MB, NB), 1)
    sub = lax.broadcasted_iota(jnp.int32, (MB, NB), 0)
    sub1 = lax.broadcasted_iota(jnp.int32, (MB, 128), 0)
    own = (lane >= r0) & (lane < r0 + MB)
    blk = w_ref[r0:r0 + MB, :]
    d = blk[:, r0:r0 + MB]
    rep = {(i, j): jnp.broadcast_to(d[i:i + 1, j:j + 1], (MB, 128)) for i in range(MB) for j in range(i + 1)}
    low, inv = {}, {}
    a = dict(rep)
    rs = []
    for j in range(MB):
        r = lax.rsqrt(a[j, j])
        rs.append(r)
        for i in range(j + 1, MB):
            low[i, j] = a[i, j] * r
        for k in range(j + 1, MB):
            for i in range(k, MB):
                a[i, k] = a[i, k] - low[i, j] * low[k, j]
    for j in range(MB):
        inv[j, j] = rs[j]
        for i in range(j + 1, MB):
            t = low[i, j] * inv[j, j]
            for k in range(j + 1, i):
                t = t + low[i, k] * inv[k, j]
            inv[i, j] = -t * rs[i]
    ainv = {}
    for i in range(MB):
        for j in range(i + 1):
            t = inv[i, i] * inv[i, j]
            for k in range(i + 1, MB):
                t = t + inv[k, i] * inv[k, j]
            ainv[i, j] = ainv[j, i] = t
    aug = []
    for j in range(MB):
        row = jnp.broadcast_to(w_ref[r0 + j:r0 + j + 1, :], (MB, NB))
        aug.append(jnp.where(own, jnp.where(lane == r0 + j, 1.0, 0.0), row))
    def mix(coef, lower):
        out = None
        for j in range(MB):
            col = jnp.zeros((MB, 128), jnp.float32)
            for i in range(j if lower else 0, MB):
                col = jnp.where(sub1 == i, coef[i, j], col)
            term = jnp.concatenate([col, col], axis=1) * aug[j]
            out = term if out is None else out + term
        return out
    z = mix(ainv, False)
    if pend > r0 + MB:
        rows = w_ref[r0 + MB:pend, :]
        n = pend - r0 - MB
        lane_n = lax.broadcasted_iota(jnp.int32, (n, NB), 1)
        acc = jnp.where((lane_n >= r0) & (lane_n < r0 + MB), 0.0, rows)
        for j in range(MB):
            acc = acc - rows[:, r0 + j:r0 + j + 1] * z[j:j + 1, :]
        w_ref[r0 + MB:pend, :] = acc
    w_ref[r0:r0 + MB, :] = mix(inv, True)

def panel(w_ref, kb):
    p0 = kb * PB
    for m in range(PB // MB):
        micro(w_ref, p0 + m * MB, p0 + PB)
    if p0 + PB < NB:
        r = w_ref[p0:p0 + PB, :]
        n = NB - p0 - PB
        lane_r = lax.broadcasted_iota(jnp.int32, (PB, NB), 1)
        sub_r = lax.broadcasted_iota(jnp.int32, (PB, NB), 0) + p0
        solved = jnp.where((lane_r > sub_r) & (lane_r < p0 + PB), 0.0, r)
        rest = w_ref[p0 + PB:NB, :]
        lane_n = lax.broadcasted_iota(jnp.int32, (n, NB), 1)
        rest = jnp.where((lane_n >= p0) & (lane_n < p0 + PB), 0.0, rest)
        up = lax.dot_general(r[:, p0 + PB:NB], solved, (((0,), (0,)), ((), ())), precision=HI, preferred_element_type=jnp.float32)
        w_ref[p0 + PB:NB, :] = rest - up

def inv_rows(w_ref, kb):
    p0 = kb * PB
    x = w_ref[p0:p0 + PB, :]
    lane = lax.broadcasted_iota(jnp.int32, (PB, NB), 1)
    sub = lax.broadcasted_iota(jnp.int32, (PB, NB), 0) + p0
    return jnp.where(lane <= sub, x, 0.0)


def gather_kernel(a_ref, r_ref, c_ref, i_ref, a_v, w_ref, inv_v, load_sem, send_sem, ysend_sem, csend_sem, r_sem, i_sem, s_sem, g_sem):
    p, q = lax.axis_index("prow"), lax.axis_index("pcol")
    x, y, z, c = lax.rem(p, 4), p // 4, q // 2, lax.rem(q, 2)
    source = q == 0
    owner = jnp.logical_and(p == 0, source)
    bar = pltpu.get_barrier_semaphore()

    def greet(row, col):
        pl.semaphore_signal(bar, 1, device_id=(row, col), device_id_type=MESH)

    def remote(ref, send, recv, row, col):
        return pltpu.make_async_remote_copy(src_ref=ref, dst_ref=ref, send_sem=send, recv_sem=recv, device_id=(row, col), device_id_type=MESH)

    def wait(ref, sem):
        pltpu.make_async_copy(ref, ref, sem).wait()

    def r_chunk(n):
        return r_ref.at[n // PER, pl.ds((n % PER) * ROWS, ROWS), :]

    def i_chunk(m):
        return i_ref.at[pl.ds(m * ROWS, ROWS), :]

    @pl.loop(1, 16)
    def _(d):
        greet(lax.rem(p + d, 16), q)

    @pl.when(jnp.logical_not(owner))
    def _():
        greet(q, 0)

    for kid, parents in ((1, (2,)), (2, (0,)), (3, (2,)), (4, (3, 5)), (5, (6,)), (6, (0,)), (7, (6,))):
        @pl.when(jnp.logical_and(c == 0, z == kid))
        def _(parents=parents):
            for parent in parents:
                greet(p, 2 * parent)

    @pl.when(c == 1)
    def _():
        greet(p, q - 1)

    @pl.when(jnp.logical_and(source, y != 0))
    def _():
        greet(x, 0)

    @pl.when(jnp.logical_and(source, jnp.logical_and(y == 0, x != 0)))
    def _():
        greet(0, 0)

    one = lambda cond: jnp.where(cond, 1, 0)
    near = one(c == 0)
    kids = near + 2 * near * (one(z == 0) + one(z == 2) + one(z == 6)) + near * (one(z == 3) + one(z == 5))
    expect = 15 + one(source) * (16 - one(owner)) + kids + 3 * one(jnp.logical_and(source, y == 0)) + 3 * one(owner)

    def greeted():
        pl.semaphore_wait(bar, expect)

    def pass_on(ref, recv, kids):
        for slot, kid in enumerate(kids):
            remote(ref, send_sem.at[slot], recv, p, 2 * kid).start()
        remote(ref, send_sem.at[2], recv, p, q + 1).start()

    def scatter(t):
        @pl.loop(0, 16)
        def _(s):
            part = pl.ds(pl.multiple_of(s * SL, SL), SL)

            @pl.when(jnp.logical_or(s != 0, jnp.logical_not(owner)))
            def _():
                pltpu.make_async_remote_copy(
                    src_ref=r_ref.at[t, part, :], dst_ref=c_ref.at[t, part, :], send_sem=csend_sem.at[0],
                    recv_sem=s_sem.at[t], device_id=(s, p), device_id_type=MESH).start()

            @pl.when(jnp.logical_and(s == 0, owner))
            def _():
                pltpu.make_async_copy(r_ref.at[t, pl.ds(0, SL), :], c_ref.at[t, pl.ds(0, SL), :], s_sem.at[t]).start()

    mine = pl.ds(pl.multiple_of(p * SL, SL), SL)

    def share(t):
        wait(c_ref.at[t, mine, :], s_sem.at[t])

        @pl.loop(1, 16)
        def _(d):
            remote(c_ref.at[t, mine, :], csend_sem.at[1], g_sem.at[t], lax.rem(p + d, 16), q).start()

    def load(t):
        return pltpu.make_async_copy(a_ref.at[t, 0, :, 0, 0, :], r_ref.at[t], load_sem.at[t])

    @pl.when(owner)
    def _():
        first = pltpu.make_async_copy(a_ref.at[0, 0, :, 0, 0, :], a_v, load_sem.at[0])
        first.start()
        for t in range(1, T):
            load(t).start()
        first.wait()
        a = a_v[...]
        w_ref[...] = 0.5 * (a + a.T)
        a_v[...] = w_ref[...]
        kept = pltpu.make_async_copy(a_v, r_ref.at[0], load_sem.at[0])
        kept.start()
        for kb in range(3):
            panel(w_ref, kb)
            inv_v[kb * PB:(kb + 1) * PB, :] = inv_rows(w_ref, kb)
        kept.wait()
        for t in range(1, T):
            load(t).wait()
        greeted()

        def give(m):
            part = pl.ds(m * ROWS, ROWS)
            src = inv_v.at[part, :]
            to = [(1, 0, 0), (2, 0, 1), (3, 0, 2), (4, 0, 3), (8, 0, 4), (12, 0, 5)]
            for row, col, slot in to:
                pltpu.make_async_remote_copy(src_ref=src, dst_ref=i_chunk(m), send_sem=ysend_sem.at[slot], recv_sem=i_sem.at[m], device_id=(row, col), device_id_type=MESH).start()
            for col, slot in ((4, 0), (12, 1), (1, 2)):
                pltpu.make_async_remote_copy(src_ref=src, dst_ref=i_chunk(m), send_sem=send_sem.at[slot], recv_sem=i_sem.at[m], device_id=(0, col), device_id_type=MESH).start()
            pltpu.make_async_copy(src, i_chunk(m), i_sem.at[m]).start()

        for m in range(3):
            give(m)
        for t in range(T):
            for n in range(PER * t, PER * t + PER):
                pass_on(r_chunk(n), r_sem.at[n], (2, 6))
            scatter(t)
        panel(w_ref, 3)
        inv_v[3 * PB:4 * PB, :] = inv_rows(w_ref, 3)
        give(3)
        for t in range(T):
            share(t)
        for m in range(4):
            wait(i_chunk(m), i_sem.at[m])

    @pl.when(jnp.logical_and(source, jnp.logical_not(owner)))
    def _():
        for t in range(T):
            load(t).start()
        for t in range(T):
            load(t).wait()
        greeted()
        for t in range(T):
            for n in range(PER * t, PER * t + PER):
                pass_on(r_chunk(n), r_sem.at[n], (2, 6))
            scatter(t)
        for m in range(4):
            wait(i_chunk(m), i_sem.at[m])

            @pl.when(y == 0)
            def _():
                for k in range(1, 4):
                    remote(i_chunk(m), ysend_sem.at[k - 1], i_sem.at[m], 4 * k + x, 0).start()
            pass_on(i_chunk(m), i_sem.at[m], (2, 6))
        for t in range(T):
            share(t)

    @pl.when(q != 0)
    def _():
        greeted()

    def relay(ref, sem, n):
        wait(ref, sem)

        @pl.when(z == 2)
        def _():
            for slot, kid in enumerate((1, 3)):
                remote(ref, send_sem.at[slot], sem, p, 2 * kid).start()

        @pl.when(z == 6)
        def _():
            for slot, kid in enumerate((5, 7)):
                remote(ref, send_sem.at[slot], sem, p, 2 * kid).start()

        @pl.when(z == (3 if n % 2 == 0 else 5))
        def _():
            remote(ref, send_sem.at[0], sem, p, 8).start()
        remote(ref, send_sem.at[2], sem, p, q + 1).start()

    @pl.when(jnp.logical_and(c == 0, z != 0))
    def _():
        for t in range(T):
            for n in range(PER * t, PER * t + PER):
                relay(r_chunk(n), r_sem.at[n], n)
            share(t)
        for m in range(4):
            relay(i_chunk(m), i_sem.at[m], m)

    @pl.when(c == 1)
    def _():
        for t in range(T):
            share(t)
        for n in range(T * PER):
            wait(r_chunk(n), r_sem.at[n])
        for m in range(4):
            wait(i_chunk(m), i_sem.at[m])

    for t in range(T):
        wait(c_ref.at[t, pl.ds(0, NB - SL), :], g_sem.at[t])
    wait(c_ref.at[:, pl.ds(0, NB - SL), :], csend_sem.at[1])

    @pl.when(owner)
    def _():
        wait(c_ref.at[:, pl.ds(0, NB - SL), :], csend_sem.at[0])

    @pl.when(jnp.logical_and(source, jnp.logical_not(owner)))
    def _():
        wait(c_ref, csend_sem.at[0])

    @pl.when(jnp.logical_and(source, y == 0))
    def _():
        for k in range(3):
            wait(i_ref, ysend_sem.at[k])

    @pl.when(owner)
    def _():
        for k in range(3, 6):
            wait(i_ref, ysend_sem.at[k])

    def sent(slot):
        wait(r_ref, send_sem.at[slot])
        wait(i_ref, send_sem.at[slot])

    @pl.when(c == 0)
    def _():
        sent(2)

    @pl.when(jnp.logical_and(c == 0, jnp.logical_or(z == 0, jnp.logical_or(z == 2, z == 6))))
    def _():
        sent(0)
        sent(1)

    @pl.when(jnp.logical_and(c == 0, jnp.logical_or(z == 3, z == 5)))
    def _():
        wait(r_ref.at[:, pl.ds(0, NB // 2), :], send_sem.at[0])
        wait(i_ref.at[pl.ds(0, NB // 2), :], send_sem.at[0])


def gather(matrix):
    tiles = jax.ShapeDtypeStruct((T, NB, NB), jnp.float32)
    square = jax.ShapeDtypeStruct((NB, NB), jnp.float32)
    dma = pltpu.SemaphoreType.DMA
    return pl.pallas_call(
        gather_kernel,
        out_shape=(tiles, tiles, square),
        in_specs=[pl.BlockSpec(memory_space=pltpu.HBM)],
        out_specs=[pl.BlockSpec(memory_space=pl.ANY)] * 3,
        scratch_shapes=[
            pltpu.VMEM((NB, NB), jnp.float32), pltpu.VMEM((NB, NB), jnp.float32), pltpu.VMEM((NB, NB), jnp.float32),
            dma((T,)), dma((3,)), dma((6,)), dma((2,)), dma((T * PER,)), dma((4,)), dma((T,)), dma((T,)),
        ],
        compiler_params=pltpu.CompilerParams(collective_id=0, has_side_effects=True, vmem_limit_bytes=50 * 2**20),
        name="gather",
    )(matrix)


def split(v):
    high = v.astype(jnp.bfloat16)
    return high, (v - high.astype(jnp.float32)).astype(jnp.bfloat16)


def left_parts(v):
    high, low = split(v)
    return jnp.concatenate([high, high, low], axis=1)


def right_parts(v):
    high, low = split(v)
    return jnp.concatenate([high, low, high], axis=1)


def times(left, right):
    return lax.dot_general(left, right, (((1,), (1,)), ((), ())), preferred_element_type=jnp.float32)


LANES = 128
STRIDE = T * NB // LANES
ROW_LINES = NB * STRIDE


def update_kernel(a_ref, r_ref, c_ref, i_ref, o_ref, o_v, x_v, inv3, r3, c3, store_sem):
    p, q = lax.axis_index("prow"), lax.axis_index("pcol")

    def lines(k, j, h):
        return pl.ds(k * ROW_LINES + j * (NB // LANES) + h, NB, stride=STRIDE)

    def put(k, j, v):
        for h in range(NB // LANES):
            o_v[lines(k, j, h), :] = v[:, h * LANES:(h + 1) * LANES]

    def store(k):
        part = pl.ds(k * ROW_LINES, ROW_LINES)
        return pltpu.make_async_copy(o_v.at[part, :], o_ref.at[part, :], store_sem.at[k])

    inv3[...] = right_parts(i_ref[...])
    for k in range(T):
        c3[k] = right_parts(times(left_parts(c_ref[k]), inv3[...]))
    for k in range(T):
        v = times(left_parts(r_ref[k]), inv3[...])
        r3[k] = left_parts(v)
        x_v[...] = v
        if k == 0:
            @pl.when(jnp.logical_and(p == 0, q == 0))
            def _():
                row = lax.broadcasted_iota(jnp.int32, (NB, NB), 0)
                col = lax.broadcasted_iota(jnp.int32, (NB, NB), 1)
                x_v[...] = jnp.where(col <= row, x_v[...], 0.0)
        for j in range(T):
            if j > k:
                put(k, j, jnp.zeros((NB, NB), jnp.float32))
                continue
            a = jnp.concatenate([a_ref[lines(k, j, h), :] for h in range(NB // LANES)], axis=1)
            v = a - times(r3[k], c3[j])
            if k == j:
                v = jnp.where(p >= q, v, 0.0)
            if j == 0:
                v = jnp.where(q == 0, x_v[...], v)
            put(k, j, v)
        store(k).start()
    for k in range(T):
        store(k).wait()


def update(matrix, r, c, i):
    vmem = pl.BlockSpec(memory_space=pltpu.VMEM)
    flat = (matrix.size // LANES, LANES)
    thirds = pltpu.VMEM((T, NB, 3 * NB), jnp.bfloat16)
    out = pl.pallas_call(
        update_kernel,
        out_shape=jax.ShapeDtypeStruct(flat, jnp.float32),
        in_specs=[vmem, vmem, vmem, vmem],
        out_specs=pl.BlockSpec(memory_space=pl.ANY),
        scratch_shapes=[
            pltpu.VMEM(flat, jnp.float32), pltpu.VMEM((NB, NB), jnp.float32), pltpu.VMEM((NB, 3 * NB), jnp.bfloat16), thirds, thirds,
            pltpu.SemaphoreType.DMA((T,)),
        ],
        compiler_params=pltpu.CompilerParams(vmem_limit_bytes=32 * 2**20),
        name="update",
    )(matrix.reshape(flat), r, c, i)
    return out.reshape(matrix.shape)


def per_device(matrix):
    r, c, i = gather(matrix)
    return update(matrix, r, c, i)


def solution(mesh):
    spec = P(None, "prow", None, None, "pcol", None)
    return jax.shard_map(per_device, mesh=mesh, in_specs=(spec,), out_specs=spec, check_vma=False)
```

```python
import functools

import jax
import jax.numpy as jnp
from jax import lax
from jax.experimental import pallas as pl
from jax.experimental.pallas import tpu as pltpu
from jax.sharding import PartitionSpec as P

MESH = pl.DeviceIdType.MESH
HI = lax.Precision.HIGHEST
NB, PB, MB = 256, 64, 8
T = 5
ROWS = 64
PER = NB // ROWS
SL = 16


def micro(w_ref, r0, pend):
    lane = lax.broadcasted_iota(jnp.int32, (MB, NB), 1)
    sub = lax.broadcasted_iota(jnp.int32, (MB, NB), 0)
    sub1 = lax.broadcasted_iota(jnp.int32, (MB, 128), 0)
    own = (lane >= r0) & (lane < r0 + MB)
    blk = w_ref[r0:r0 + MB, :]
    d = blk[:, r0:r0 + MB]
    rep = {(i, j): jnp.broadcast_to(d[i:i + 1, j:j + 1], (MB, 128)) for i in range(MB) for j in range(i + 1)}
    low, inv = {}, {}
    a = dict(rep)
    rs = []
    for j in range(MB):
        r = lax.rsqrt(a[j, j])
        rs.append(r)
        for i in range(j + 1, MB):
            low[i, j] = a[i, j] * r
        for k in range(j + 1, MB):
            for i in range(k, MB):
                a[i, k] = a[i, k] - low[i, j] * low[k, j]
    for j in range(MB):
        inv[j, j] = rs[j]
        for i in range(j + 1, MB):
            t = low[i, j] * inv[j, j]
            for k in range(j + 1, i):
                t = t + low[i, k] * inv[k, j]
            inv[i, j] = -t * rs[i]
    ainv = {}
    for i in range(MB):
        for j in range(i + 1):
            t = inv[i, i] * inv[i, j]
            for k in range(i + 1, MB):
                t = t + inv[k, i] * inv[k, j]
            ainv[i, j] = ainv[j, i] = t
    aug = []
    for j in range(MB):
        row = jnp.broadcast_to(w_ref[r0 + j:r0 + j + 1, :], (MB, NB))
        aug.append(jnp.where(own, jnp.where(lane == r0 + j, 1.0, 0.0), row))
    def mix(coef, lower):
        out = None
        for j in range(MB):
            col = jnp.zeros((MB, 128), jnp.float32)
            for i in range(j if lower else 0, MB):
                col = jnp.where(sub1 == i, coef[i, j], col)
            term = jnp.concatenate([col, col], axis=1) * aug[j]
            out = term if out is None else out + term
        return out
    z = mix(ainv, False)
    if pend > r0 + MB:
        rows = w_ref[r0 + MB:pend, :]
        n = pend - r0 - MB
        lane_n = lax.broadcasted_iota(jnp.int32, (n, NB), 1)
        acc = jnp.where((lane_n >= r0) & (lane_n < r0 + MB), 0.0, rows)
        for j in range(MB):
            acc = acc - rows[:, r0 + j:r0 + j + 1] * z[j:j + 1, :]
        w_ref[r0 + MB:pend, :] = acc
    w_ref[r0:r0 + MB, :] = mix(inv, True)

def panel(w_ref, kb):
    p0 = kb * PB
    for m in range(PB // MB):
        micro(w_ref, p0 + m * MB, p0 + PB)
    if p0 + PB < NB:
        r = w_ref[p0:p0 + PB, :]
        n = NB - p0 - PB
        lane_r = lax.broadcasted_iota(jnp.int32, (PB, NB), 1)
        sub_r = lax.broadcasted_iota(jnp.int32, (PB, NB), 0) + p0
        solved = jnp.where((lane_r > sub_r) & (lane_r < p0 + PB), 0.0, r)
        rest = w_ref[p0 + PB:NB, :]
        lane_n = lax.broadcasted_iota(jnp.int32, (n, NB), 1)
        rest = jnp.where((lane_n >= p0) & (lane_n < p0 + PB), 0.0, rest)
        up = lax.dot_general(r[:, p0 + PB:NB], solved, (((0,), (0,)), ((), ())), precision=HI, preferred_element_type=jnp.float32)
        w_ref[p0 + PB:NB, :] = rest - up

def inv_rows(w_ref, kb):
    p0 = kb * PB
    x = w_ref[p0:p0 + PB, :]
    lane = lax.broadcasted_iota(jnp.int32, (PB, NB), 1)
    sub = lax.broadcasted_iota(jnp.int32, (PB, NB), 0) + p0
    return jnp.where(lane <= sub, x, 0.0)


ORDER = (1, 2, 3, 4, 0)
STEPS = (("r", 0), ("r", 1), ("s", 0), ("r", 2), ("s", 1), ("y", 0), ("r", 3), ("s", 2), ("y", 1), ("r", 4), ("s", 3), ("y", 2), ("s", 4), ("y", 3), ("y", 4), ("i", 0), ("i", 1), ("i", 2), ("i", 3))


def gather_kernel(a_ref, r_ref, c_ref, i_ref, a_v, w_ref, inv_v, load_sem, send_sem, ysend_sem, csend_sem, r_sem, i_sem, s_sem, x_sem, g_sem):
    p, q = lax.axis_index("prow"), lax.axis_index("pcol")
    x, y, z, c = lax.rem(p, 4), p // 4, q // 2, lax.rem(q, 2)
    both = jnp.logical_and
    source = q == 0
    owner = both(p == 0, source)
    plain_source = both(p != 0, source)
    lead = p == q
    first, second = c == 0, c == 1
    spread = both(q == 1, both(y == 0, x != 0))
    beside_owner = both(q == 1, p == 0)
    bar = pltpu.get_barrier_semaphore()

    def greet(row, col):
        pl.semaphore_signal(bar, 1, device_id=(row, col), device_id_type=MESH)

    def remote(ref, send, recv, row, col):
        return pltpu.make_async_remote_copy(src_ref=ref, dst_ref=ref, send_sem=send, recv_sem=recv, device_id=(row, col), device_id_type=MESH)

    def wait(ref, sem):
        pltpu.make_async_copy(ref, ref, sem).wait()

    def r_chunk(n):
        return r_ref.at[n // PER, pl.ds((n % PER) * ROWS, ROWS), :]

    def i_chunk(m):
        return i_ref.at[pl.ds(m * ROWS, ROWS), :]

    for d in range(1, 4):
        greet(4 * y + lax.rem(x + d, 4), q)
        greet(4 * lax.rem(y + d, 4) + x, q)

    @pl.when(jnp.logical_not(lead))
    def _():
        greet(q, q)

    for kid, parents in ((1, (2,)), (2, (0,)), (3, (2,)), (4, (3, 5)), (5, (6,)), (6, (0,)), (7, (6,))):
        @pl.when(z == kid)
        def _(parents=parents):
            for parent in parents:
                greet(p, 2 * parent + c)

    @pl.when(second)
    def _():
        greet(p, q - 1)

    @pl.when(both(first, jnp.logical_not(owner)))
    def _():
        greet(p, q + 1)

    @pl.when(q == 1)
    def _():
        @pl.when(both(x != 0, y != 0))
        def _():
            greet(x, 1)

        @pl.when(jnp.logical_or(x == 0, y == 0))
        def _():
            greet(0, 0)

    one = lambda cond: jnp.where(cond, 1, 0)
    along = 2 * (one(z == 0) + one(z == 2) + one(z == 6)) + one(z == 3) + one(z == 5)
    expect = 6 + 15 * one(lead) + along + 1 - one(beside_owner) + 3 * one(spread) + 7 * one(owner)

    def greeted():
        pl.semaphore_wait(bar, expect)

    def pass_z(ref, sem, n):
        for parent, kids in ((0, (2, 6)), (2, (1, 3)), (6, (5, 7)), (3 if n % 2 == 0 else 5, (4,))):
            @pl.when(z == parent)
            def _(kids=kids):
                for slot, kid in enumerate(kids):
                    remote(ref, send_sem.at[slot], sem, p, 2 * kid + c).start()

    def send_r(t):
        for n in range(PER * t, PER * t + PER):
            pass_z(r_chunk(n), r_sem.at[n], n)
            remote(r_chunk(n), send_sem.at[2], r_sem.at[n], p, q + 1).start()

    def relay_i(m):
        wait(i_chunk(m), i_sem.at[m])

        @pl.when(spread)
        def _():
            for k in range(1, 4):
                remote(i_chunk(m), ysend_sem.at[k - 1], i_sem.at[m], 4 * k + x, 1).start()
        pass_z(i_chunk(m), i_sem.at[m], m)

        @pl.when(jnp.logical_not(beside_owner))
        def _():
            remote(i_chunk(m), send_sem.at[2], i_sem.at[m], p, q - 1).start()

    mine = pl.ds(pl.multiple_of(p * SL, SL), SL)

    def scatter(t):
        @pl.loop(1, 16)
        def _(d):
            row = lax.rem(p + d, 16)
            part = pl.ds(pl.multiple_of(row * SL, SL), SL)
            pltpu.make_async_remote_copy(
                src_ref=r_ref.at[t, part, :], dst_ref=c_ref.at[t, part, :], send_sem=csend_sem.at[0],
                recv_sem=s_sem.at[t], device_id=(row, q), device_id_type=MESH).start()
        pltpu.make_async_copy(r_ref.at[t, mine, :], c_ref.at[t, mine, :], s_sem.at[t]).start()

    def share(t):
        wait(c_ref.at[t, mine, :], s_sem.at[t])
        for d in range(1, 4):
            remote(c_ref.at[t, mine, :], csend_sem.at[1], x_sem.at[t], 4 * y + lax.rem(x + d, 4), q).start()

    def share_y(t):
        wait(c_ref.at[t, pl.ds(0, 3 * SL), :], x_sem.at[t])
        ours = c_ref.at[t, pl.ds(pl.multiple_of(y * 4 * SL, 4 * SL), 4 * SL), :]
        for d in range(1, 4):
            remote(ours, csend_sem.at[2], g_sem.at[t], 4 * lax.rem(y + d, 4) + x, q).start()

    def load(t):
        return pltpu.make_async_copy(a_ref.at[t, 0, :, 0, 0, :], r_ref.at[t], load_sem.at[t])

    def factor(kb):
        panel(w_ref, kb)
        inv_v[kb * PB:(kb + 1) * PB, :] = inv_rows(w_ref, kb)

    def give(m):
        src = inv_v.at[pl.ds(m * ROWS, ROWS), :]
        for slot, row in enumerate((1, 2, 3, 4, 8, 12, 0)):
            pltpu.make_async_remote_copy(src_ref=src, dst_ref=i_chunk(m), send_sem=ysend_sem.at[slot], recv_sem=i_sem.at[m], device_id=(row, 1), device_id_type=MESH).start()
        pltpu.make_async_copy(src, i_chunk(m), i_sem.at[m]).start()

    @pl.when(owner)
    def _():
        lead_tile = pltpu.make_async_copy(a_ref.at[0, 0, :, 0, 0, :], a_v, load_sem.at[0])
        lead_tile.start()
        for t in range(1, T):
            load(t).start()
        lead_tile.wait()
        a = a_v[...]
        w_ref[...] = 0.5 * (a + a.T)
        a_v[...] = w_ref[...]
        kept = pltpu.make_async_copy(a_v, r_ref.at[0], load_sem.at[0])
        kept.start()
        factor(0)
        factor(1)
        kept.wait()
        for t in range(1, T):
            load(t).wait()
        greeted()
        give(0)
        give(1)
        for t in (1, 2):
            send_r(t)
            scatter(t)
        factor(2)
        give(2)
        send_r(3)
        scatter(3)
        factor(3)
        give(3)
        for t in (4, 0):
            send_r(t)
            scatter(t)

    @pl.when(plain_source)
    def _():
        for t in ORDER:
            load(t).start()
        greeted()
        for t in ORDER:
            load(t).wait()
            send_r(t)

    @pl.when(source)
    def _():
        for n, t in enumerate(ORDER):
            share(t)
            if n > 0:
                share_y(ORDER[n - 1])
        share_y(ORDER[-1])

    @pl.when(q != 0)
    def _():
        greeted()

    def take(t):
        for n in range(PER * t, PER * t + PER):
            wait(r_chunk(n), r_sem.at[n])

            @pl.when(first)
            def _(n=n):
                pass_z(r_chunk(n), r_sem.at[n], n)
                remote(r_chunk(n), send_sem.at[2], r_sem.at[n], p, q + 1).start()

        @pl.when(lead)
        def _():
            scatter(t)

    @pl.when(q != 0)
    def _():
        for step in STEPS:
            kind, n = step
            if kind == "r":
                take(ORDER[n])
            elif kind == "s":
                share(ORDER[n])
            elif kind == "y":
                share_y(ORDER[n])
            else:
                pl.when(second)(functools.partial(relay_i, n))

    @pl.when(first)
    def _():
        for m in range(4):
            wait(i_chunk(m), i_sem.at[m])
    for t in ORDER:
        wait(c_ref.at[t, pl.ds(0, NB - 4 * SL), :], g_sem.at[t])
    wait(c_ref.at[:, pl.ds(0, 3 * SL), :], csend_sem.at[1])
    wait(c_ref.at[:, pl.ds(0, NB - 4 * SL), :], csend_sem.at[2])

    @pl.when(lead)
    def _():
        wait(c_ref.at[:, pl.ds(0, NB - SL), :], csend_sem.at[0])

    @pl.when(owner)
    def _():
        for k in range(7):
            wait(i_ref, ysend_sem.at[k])

    @pl.when(spread)
    def _():
        for k in range(3):
            wait(i_ref, ysend_sem.at[k])

    wide = jnp.logical_or(z == 0, jnp.logical_or(z == 2, z == 6))
    half = jnp.logical_or(z == 3, z == 5)

    @pl.when(first)
    def _():
        wait(r_ref, send_sem.at[2])

        @pl.when(wide)
        def _():
            wait(r_ref, send_sem.at[0])
            wait(r_ref, send_sem.at[1])

        @pl.when(half)
        def _():
            wait(r_ref.at[:, pl.ds(0, NB // 2), :], send_sem.at[0])

    @pl.when(second)
    def _():
        @pl.when(jnp.logical_not(beside_owner))
        def _():
            wait(i_ref, send_sem.at[2])

        @pl.when(wide)
        def _():
            wait(i_ref, send_sem.at[0])
            wait(i_ref, send_sem.at[1])

        @pl.when(half)
        def _():
            wait(i_ref.at[pl.ds(0, NB // 2), :], send_sem.at[0])


def gather(matrix):
    tiles = jax.ShapeDtypeStruct((T, NB, NB), jnp.float32)
    square = jax.ShapeDtypeStruct((NB, NB), jnp.float32)
    dma = pltpu.SemaphoreType.DMA
    return pl.pallas_call(
        gather_kernel,
        out_shape=(tiles, tiles, square),
        in_specs=[pl.BlockSpec(memory_space=pltpu.HBM)],
        out_specs=[pl.BlockSpec(memory_space=pl.ANY)] * 3,
        scratch_shapes=[
            pltpu.VMEM((NB, NB), jnp.float32), pltpu.VMEM((NB, NB), jnp.float32), pltpu.VMEM((NB, NB), jnp.float32),
            dma((T,)), dma((3,)), dma((7,)), dma((3,)), dma((T * PER,)), dma((4,)), dma((T,)), dma((T,)), dma((T,)),
        ],
        compiler_params=pltpu.CompilerParams(collective_id=0, has_side_effects=True, vmem_limit_bytes=50 * 2**20),
        name="gather",
    )(matrix)


def split(v):
    high = v.astype(jnp.bfloat16)
    return high, (v - high.astype(jnp.float32)).astype(jnp.bfloat16)


def left_parts(v):
    high, low = split(v)
    return jnp.concatenate([high, high, low], axis=1)


def right_parts(v):
    high, low = split(v)
    return jnp.concatenate([high, low, high], axis=1)


def times(left, right):
    return lax.dot_general(left, right, (((1,), (1,)), ((), ())), preferred_element_type=jnp.float32)


LANES = 128
STRIDE = T * NB // LANES
ROW_LINES = NB * STRIDE


def update_kernel(a_ref, r_ref, c_ref, i_ref, o_ref, o_v, x_v, inv3, r3, c3, store_sem):
    p, q = lax.axis_index("prow"), lax.axis_index("pcol")

    def lines(k, j, h):
        return pl.ds(k * ROW_LINES + j * (NB // LANES) + h, NB, stride=STRIDE)

    def put(k, j, v):
        for h in range(NB // LANES):
            o_v[lines(k, j, h), :] = v[:, h * LANES:(h + 1) * LANES]

    def store(k):
        part = pl.ds(k * ROW_LINES, ROW_LINES)
        return pltpu.make_async_copy(o_v.at[part, :], o_ref.at[part, :], store_sem.at[k])

    inv3[...] = right_parts(i_ref[...])
    for k in range(T):
        c3[k] = right_parts(times(left_parts(c_ref[k]), inv3[...]))
    for k in range(T):
        v = times(left_parts(r_ref[k]), inv3[...])
        r3[k] = left_parts(v)
        x_v[...] = v
        if k == 0:
            @pl.when(jnp.logical_and(p == 0, q == 0))
            def _():
                row = lax.broadcasted_iota(jnp.int32, (NB, NB), 0)
                col = lax.broadcasted_iota(jnp.int32, (NB, NB), 1)
                x_v[...] = jnp.where(col <= row, x_v[...], 0.0)
        for j in range(T):
            if j > k:
                put(k, j, jnp.zeros((NB, NB), jnp.float32))
                continue
            a = jnp.concatenate([a_ref[lines(k, j, h), :] for h in range(NB // LANES)], axis=1)
            v = a - times(r3[k], c3[j])
            if k == j:
                v = jnp.where(p >= q, v, 0.0)
            if j == 0:
                v = jnp.where(q == 0, x_v[...], v)
            put(k, j, v)
        store(k).start()
    for k in range(T):
        store(k).wait()


def update(matrix, r, c, i):
    vmem = pl.BlockSpec(memory_space=pltpu.VMEM)
    flat = (matrix.size // LANES, LANES)
    thirds = pltpu.VMEM((T, NB, 3 * NB), jnp.bfloat16)
    out = pl.pallas_call(
        update_kernel,
        out_shape=jax.ShapeDtypeStruct(flat, jnp.float32),
        in_specs=[vmem, vmem, vmem, vmem],
        out_specs=pl.BlockSpec(memory_space=pl.ANY),
        scratch_shapes=[
            pltpu.VMEM(flat, jnp.float32), pltpu.VMEM((NB, NB), jnp.float32), pltpu.VMEM((NB, 3 * NB), jnp.bfloat16), thirds, thirds,
            pltpu.SemaphoreType.DMA((T,)),
        ],
        compiler_params=pltpu.CompilerParams(vmem_limit_bytes=32 * 2**20),
        name="update",
    )(matrix.reshape(flat), r, c, i)
    return out.reshape(matrix.shape)


def per_device(matrix):
    r, c, i = gather(matrix)
    return update(matrix, r, c, i)


def solution(mesh):
    spec = P(None, "prow", None, None, "pcol", None)
    return jax.shard_map(per_device, mesh=mesh, in_specs=(spec,), out_specs=spec, check_vma=False)
```

```python
import functools

import jax
import jax.numpy as jnp
from jax import lax
from jax.experimental import pallas as pl
from jax.experimental.pallas import tpu as pltpu
from jax.sharding import PartitionSpec as P

MESH = pl.DeviceIdType.MESH
HI = lax.Precision.HIGHEST
NB, PB, MB = 256, 64, 8
T = 5
ROWS = 64
PER = NB // ROWS
SL = 16


def micro(w_ref, r0, pend):
    lane = lax.broadcasted_iota(jnp.int32, (MB, NB), 1)
    sub = lax.broadcasted_iota(jnp.int32, (MB, NB), 0)
    sub1 = lax.broadcasted_iota(jnp.int32, (MB, 128), 0)
    own = (lane >= r0) & (lane < r0 + MB)
    blk = w_ref[r0:r0 + MB, :]
    d = blk[:, r0:r0 + MB]
    rep = {(i, j): jnp.broadcast_to(d[i:i + 1, j:j + 1], (MB, 128)) for i in range(MB) for j in range(i + 1)}
    low, inv = {}, {}
    a = dict(rep)
    rs = []
    for j in range(MB):
        r = lax.rsqrt(a[j, j])
        rs.append(r)
        for i in range(j + 1, MB):
            low[i, j] = a[i, j] * r
        for k in range(j + 1, MB):
            for i in range(k, MB):
                a[i, k] = a[i, k] - low[i, j] * low[k, j]
    for j in range(MB):
        inv[j, j] = rs[j]
        for i in range(j + 1, MB):
            t = low[i, j] * inv[j, j]
            for k in range(j + 1, i):
                t = t + low[i, k] * inv[k, j]
            inv[i, j] = -t * rs[i]
    ainv = {}
    for i in range(MB):
        for j in range(i + 1):
            t = inv[i, i] * inv[i, j]
            for k in range(i + 1, MB):
                t = t + inv[k, i] * inv[k, j]
            ainv[i, j] = ainv[j, i] = t
    aug = []
    for j in range(MB):
        row = jnp.broadcast_to(w_ref[r0 + j:r0 + j + 1, :], (MB, NB))
        aug.append(jnp.where(own, jnp.where(lane == r0 + j, 1.0, 0.0), row))
    def mix(coef, lower):
        out = None
        for j in range(MB):
            col = jnp.zeros((MB, 128), jnp.float32)
            for i in range(j if lower else 0, MB):
                col = jnp.where(sub1 == i, coef[i, j], col)
            term = jnp.concatenate([col, col], axis=1) * aug[j]
            out = term if out is None else out + term
        return out
    z = mix(ainv, False)
    if pend > r0 + MB:
        rows = w_ref[r0 + MB:pend, :]
        n = pend - r0 - MB
        lane_n = lax.broadcasted_iota(jnp.int32, (n, NB), 1)
        acc = jnp.where((lane_n >= r0) & (lane_n < r0 + MB), 0.0, rows)
        for j in range(MB):
            acc = acc - rows[:, r0 + j:r0 + j + 1] * z[j:j + 1, :]
        w_ref[r0 + MB:pend, :] = acc
    w_ref[r0:r0 + MB, :] = mix(inv, True)

def panel(w_ref, kb):
    p0 = kb * PB
    for m in range(PB // MB):
        micro(w_ref, p0 + m * MB, p0 + PB)
    if p0 + PB < NB:
        r = w_ref[p0:p0 + PB, :]
        n = NB - p0 - PB
        lane_r = lax.broadcasted_iota(jnp.int32, (PB, NB), 1)
        sub_r = lax.broadcasted_iota(jnp.int32, (PB, NB), 0) + p0
        solved = jnp.where((lane_r > sub_r) & (lane_r < p0 + PB), 0.0, r)
        rest = w_ref[p0 + PB:NB, :]
        lane_n = lax.broadcasted_iota(jnp.int32, (n, NB), 1)
        rest = jnp.where((lane_n >= p0) & (lane_n < p0 + PB), 0.0, rest)
        up = lax.dot_general(r[:, p0 + PB:NB], solved, (((0,), (0,)), ((), ())), precision=HI, preferred_element_type=jnp.float32)
        w_ref[p0 + PB:NB, :] = rest - up

def inv_rows(w_ref, kb):
    p0 = kb * PB
    x = w_ref[p0:p0 + PB, :]
    lane = lax.broadcasted_iota(jnp.int32, (PB, NB), 1)
    sub = lax.broadcasted_iota(jnp.int32, (PB, NB), 0) + p0
    return jnp.where(lane <= sub, x, 0.0)


ORDER = (1, 2, 3, 4, 0)
STEPS = (("r", 0), ("r", 1), ("s", 0), ("r", 2), ("s", 1), ("y", 0), ("r", 3), ("s", 2), ("y", 1), ("r", 4), ("s", 3), ("y", 2), ("s", 4), ("y", 3), ("y", 4), ("i", 0), ("i", 1), ("i", 2), ("i", 3))


def gather_kernel(a_ref, r_ref, c_ref, i_ref, a_v, w_ref, inv_v, load_sem, send_sem, ysend_sem, csend_sem, r_sem, i_sem, s_sem, x_sem, g_sem):
    p, q = lax.axis_index("prow"), lax.axis_index("pcol")
    x, y, z, c = lax.rem(p, 4), p // 4, q // 2, lax.rem(q, 2)
    both = jnp.logical_and
    source = q == 0
    owner = both(p == 0, source)
    plain_source = both(p != 0, source)
    lead = p == q
    first, second = c == 0, c == 1
    spread = both(q == 1, both(y == 0, x != 0))
    beside_owner = both(q == 1, p == 0)
    bar = pltpu.get_barrier_semaphore()

    def greet(row, col):
        pl.semaphore_signal(bar, 1, device_id=(row, col), device_id_type=MESH)

    def remote(ref, send, recv, row, col):
        return pltpu.make_async_remote_copy(src_ref=ref, dst_ref=ref, send_sem=send, recv_sem=recv, device_id=(row, col), device_id_type=MESH)

    def wait(ref, sem):
        pltpu.make_async_copy(ref, ref, sem).wait()

    def r_chunk(n):
        return r_ref.at[n // PER, pl.ds((n % PER) * ROWS, ROWS), :]

    def i_chunk(m):
        return i_ref.at[pl.ds(m * ROWS, ROWS), :]

    for d in range(1, 4):
        greet(4 * y + lax.rem(x + d, 4), q)
        greet(4 * lax.rem(y + d, 4) + x, q)

    @pl.when(jnp.logical_not(lead))
    def _():
        greet(q, q)

    for kid, parents in ((1, (2,)), (2, (0,)), (3, (2,)), (4, (3, 5)), (5, (6,)), (6, (0,)), (7, (6,))):
        @pl.when(z == kid)
        def _(parents=parents):
            for parent in parents:
                greet(p, 2 * parent + c)

    @pl.when(second)
    def _():
        greet(p, q - 1)

    @pl.when(both(first, jnp.logical_not(owner)))
    def _():
        greet(p, q + 1)

    @pl.when(q == 1)
    def _():
        @pl.when(both(x != 0, y != 0))
        def _():
            greet(x, 1)

        @pl.when(jnp.logical_or(x == 0, y == 0))
        def _():
            greet(0, 0)

    one = lambda cond: jnp.where(cond, 1, 0)
    along = 2 * (one(z == 0) + one(z == 2) + one(z == 6)) + one(z == 3) + one(z == 5)
    expect = 6 + 15 * one(lead) + along + 1 - one(beside_owner) + 3 * one(spread) + 7 * one(owner)

    def greeted():
        pl.semaphore_wait(bar, expect)

    def pass_z(ref, sem, n):
        for parent, kids in ((0, (2, 6)), (2, (1, 3)), (6, (5, 7)), (3 if n % 2 == 0 else 5, (4,))):
            @pl.when(z == parent)
            def _(kids=kids):
                for slot, kid in enumerate(kids):
                    remote(ref, send_sem.at[slot], sem, p, 2 * kid + c).start()

    def send_r(t):
        for n in range(PER * t, PER * t + PER):
            pass_z(r_chunk(n), r_sem.at[n], n)
            remote(r_chunk(n), send_sem.at[2], r_sem.at[n], p, q + 1).start()

    def relay_i(m):
        wait(i_chunk(m), i_sem.at[m])

        @pl.when(spread)
        def _():
            for k in range(1, 4):
                remote(i_chunk(m), ysend_sem.at[k - 1], i_sem.at[m], 4 * k + x, 1).start()
        pass_z(i_chunk(m), i_sem.at[m], m)

        @pl.when(jnp.logical_not(beside_owner))
        def _():
            remote(i_chunk(m), send_sem.at[2], i_sem.at[m], p, q - 1).start()

    mine = pl.ds(pl.multiple_of(p * SL, SL), SL)

    def scatter_part(t, j):
        for i in range(PER):
            row = PER * j + i
            part = pl.ds(row * SL, SL)

            @pl.when(p != row)
            def _(row=row, part=part):
                pltpu.make_async_remote_copy(
                    src_ref=r_ref.at[t, part, :], dst_ref=c_ref.at[t, part, :], send_sem=csend_sem.at[0],
                    recv_sem=s_sem.at[t], device_id=(row, q), device_id_type=MESH).start()

            @pl.when(p == row)
            def _(part=part):
                pltpu.make_async_copy(r_ref.at[t, part, :], c_ref.at[t, part, :], s_sem.at[t]).start()

    def scatter(t):
        for j in range(PER):
            scatter_part(t, j)

    def share(t):
        wait(c_ref.at[t, mine, :], s_sem.at[t])
        for d in range(1, 4):
            remote(c_ref.at[t, mine, :], csend_sem.at[1], x_sem.at[t], 4 * y + lax.rem(x + d, 4), q).start()

    def share_y(t):
        wait(c_ref.at[t, pl.ds(0, 3 * SL), :], x_sem.at[t])
        ours = c_ref.at[t, pl.ds(pl.multiple_of(y * 4 * SL, 4 * SL), 4 * SL), :]
        for d in range(1, 4):
            remote(ours, csend_sem.at[2], g_sem.at[t], 4 * lax.rem(y + d, 4) + x, q).start()

    def load(t):
        return pltpu.make_async_copy(a_ref.at[t, 0, :, 0, 0, :], r_ref.at[t], load_sem.at[t])

    def factor(kb):
        panel(w_ref, kb)
        inv_v[kb * PB:(kb + 1) * PB, :] = inv_rows(w_ref, kb)

    def give(m):
        src = inv_v.at[pl.ds(m * ROWS, ROWS), :]
        for slot, row in enumerate((1, 2, 3, 4, 8, 12, 0)):
            pltpu.make_async_remote_copy(src_ref=src, dst_ref=i_chunk(m), send_sem=ysend_sem.at[slot], recv_sem=i_sem.at[m], device_id=(row, 1), device_id_type=MESH).start()
        pltpu.make_async_copy(src, i_chunk(m), i_sem.at[m]).start()

    @pl.when(owner)
    def _():
        lead_tile = pltpu.make_async_copy(a_ref.at[0, 0, :, 0, 0, :], a_v, load_sem.at[0])
        lead_tile.start()
        for t in range(1, T):
            load(t).start()
        lead_tile.wait()
        a = a_v[...]
        w_ref[...] = 0.5 * (a + a.T)
        a_v[...] = w_ref[...]
        kept = pltpu.make_async_copy(a_v, r_ref.at[0], load_sem.at[0])
        kept.start()
        factor(0)
        factor(1)
        kept.wait()
        for t in range(1, T):
            load(t).wait()
        greeted()
        give(0)
        give(1)
        for t in (1, 2):
            send_r(t)
            scatter(t)
        factor(2)
        give(2)
        send_r(3)
        scatter(3)
        factor(3)
        give(3)
        for t in (4, 0):
            send_r(t)
            scatter(t)

    @pl.when(plain_source)
    def _():
        for t in ORDER:
            load(t).start()
        greeted()
        for t in ORDER:
            load(t).wait()
            send_r(t)

    @pl.when(source)
    def _():
        for n, t in enumerate(ORDER):
            share(t)
            if n > 0:
                share_y(ORDER[n - 1])
        share_y(ORDER[-1])

    @pl.when(q != 0)
    def _():
        greeted()

    def take(t):
        for n in range(PER * t, PER * t + PER):
            wait(r_chunk(n), r_sem.at[n])

            @pl.when(first)
            def _(n=n):
                pass_z(r_chunk(n), r_sem.at[n], n)
                remote(r_chunk(n), send_sem.at[2], r_sem.at[n], p, q + 1).start()

            @pl.when(lead)
            def _(n=n):
                scatter_part(t, n % PER)

    @pl.when(q != 0)
    def _():
        for step in STEPS:
            kind, n = step
            if kind == "r":
                take(ORDER[n])
            elif kind == "s":
                share(ORDER[n])
            elif kind == "y":
                share_y(ORDER[n])
            else:
                pl.when(second)(functools.partial(relay_i, n))

    @pl.when(first)
    def _():
        for m in range(4):
            wait(i_chunk(m), i_sem.at[m])
    for t in ORDER:
        wait(c_ref.at[t, pl.ds(0, NB - 4 * SL), :], g_sem.at[t])
    wait(c_ref.at[:, pl.ds(0, 3 * SL), :], csend_sem.at[1])
    wait(c_ref.at[:, pl.ds(0, NB - 4 * SL), :], csend_sem.at[2])

    @pl.when(lead)
    def _():
        wait(c_ref.at[:, pl.ds(0, NB - SL), :], csend_sem.at[0])

    @pl.when(owner)
    def _():
        for k in range(7):
            wait(i_ref, ysend_sem.at[k])

    @pl.when(spread)
    def _():
        for k in range(3):
            wait(i_ref, ysend_sem.at[k])

    wide = jnp.logical_or(z == 0, jnp.logical_or(z == 2, z == 6))
    half = jnp.logical_or(z == 3, z == 5)

    @pl.when(first)
    def _():
        wait(r_ref, send_sem.at[2])

        @pl.when(wide)
        def _():
            wait(r_ref, send_sem.at[0])
            wait(r_ref, send_sem.at[1])

        @pl.when(half)
        def _():
            wait(r_ref.at[:, pl.ds(0, NB // 2), :], send_sem.at[0])

    @pl.when(second)
    def _():
        @pl.when(jnp.logical_not(beside_owner))
        def _():
            wait(i_ref, send_sem.at[2])

        @pl.when(wide)
        def _():
            wait(i_ref, send_sem.at[0])
            wait(i_ref, send_sem.at[1])

        @pl.when(half)
        def _():
            wait(i_ref.at[pl.ds(0, NB // 2), :], send_sem.at[0])


def gather(matrix):
    tiles = jax.ShapeDtypeStruct((T, NB, NB), jnp.float32)
    square = jax.ShapeDtypeStruct((NB, NB), jnp.float32)
    dma = pltpu.SemaphoreType.DMA
    return pl.pallas_call(
        gather_kernel,
        out_shape=(tiles, tiles, square),
        in_specs=[pl.BlockSpec(memory_space=pltpu.HBM)],
        out_specs=[pl.BlockSpec(memory_space=pl.ANY)] * 3,
        scratch_shapes=[
            pltpu.VMEM((NB, NB), jnp.float32), pltpu.VMEM((NB, NB), jnp.float32), pltpu.VMEM((NB, NB), jnp.float32),
            dma((T,)), dma((3,)), dma((7,)), dma((3,)), dma((T * PER,)), dma((4,)), dma((T,)), dma((T,)), dma((T,)),
        ],
        compiler_params=pltpu.CompilerParams(collective_id=0, has_side_effects=True, vmem_limit_bytes=50 * 2**20),
        name="gather",
    )(matrix)


def split(v):
    high = v.astype(jnp.bfloat16)
    return high, (v - high.astype(jnp.float32)).astype(jnp.bfloat16)


def left_parts(v):
    high, low = split(v)
    return jnp.concatenate([high, high, low], axis=1)


def right_parts(v):
    high, low = split(v)
    return jnp.concatenate([high, low, high], axis=1)


def times(left, right):
    return lax.dot_general(left, right, (((1,), (1,)), ((), ())), preferred_element_type=jnp.float32)


LANES = 128
STRIDE = T * NB // LANES
ROW_LINES = NB * STRIDE


def update_kernel(a_ref, r_ref, c_ref, i_ref, o_ref, o_v, x_v, inv3, r3, c3, store_sem):
    p, q = lax.axis_index("prow"), lax.axis_index("pcol")

    def lines(k, j, h):
        return pl.ds(k * ROW_LINES + j * (NB // LANES) + h, NB, stride=STRIDE)

    def put(k, j, v):
        for h in range(NB // LANES):
            o_v[lines(k, j, h), :] = v[:, h * LANES:(h + 1) * LANES]

    def store(k):
        part = pl.ds(k * ROW_LINES, ROW_LINES)
        return pltpu.make_async_copy(o_v.at[part, :], o_ref.at[part, :], store_sem.at[k])

    inv3[...] = right_parts(i_ref[...])
    for k in range(T):
        c3[k] = right_parts(times(left_parts(c_ref[k]), inv3[...]))
    for k in range(T):
        v = times(left_parts(r_ref[k]), inv3[...])
        r3[k] = left_parts(v)
        x_v[...] = v
        if k == 0:
            @pl.when(jnp.logical_and(p == 0, q == 0))
            def _():
                row = lax.broadcasted_iota(jnp.int32, (NB, NB), 0)
                col = lax.broadcasted_iota(jnp.int32, (NB, NB), 1)
                x_v[...] = jnp.where(col <= row, x_v[...], 0.0)
        for j in range(T):
            if j > k:
                put(k, j, jnp.zeros((NB, NB), jnp.float32))
                continue
            a = jnp.concatenate([a_ref[lines(k, j, h), :] for h in range(NB // LANES)], axis=1)
            v = a - times(r3[k], c3[j])
            if k == j:
                v = jnp.where(p >= q, v, 0.0)
            if j == 0:
                v = jnp.where(q == 0, x_v[...], v)
            put(k, j, v)
        store(k).start()
    for k in range(T):
        store(k).wait()


def update(matrix, r, c, i):
    vmem = pl.BlockSpec(memory_space=pltpu.VMEM)
    flat = (matrix.size // LANES, LANES)
    thirds = pltpu.VMEM((T, NB, 3 * NB), jnp.bfloat16)
    out = pl.pallas_call(
        update_kernel,
        out_shape=jax.ShapeDtypeStruct(flat, jnp.float32),
        in_specs=[vmem, vmem, vmem, vmem],
        out_specs=pl.BlockSpec(memory_space=pl.ANY),
        scratch_shapes=[
            pltpu.VMEM(flat, jnp.float32), pltpu.VMEM((NB, NB), jnp.float32), pltpu.VMEM((NB, 3 * NB), jnp.bfloat16), thirds, thirds,
            pltpu.SemaphoreType.DMA((T,)),
        ],
        compiler_params=pltpu.CompilerParams(vmem_limit_bytes=32 * 2**20),
        name="update",
    )(matrix.reshape(flat), r, c, i)
    return out.reshape(matrix.shape)


def per_device(matrix):
    r, c, i = gather(matrix)
    return update(matrix, r, c, i)


def solution(mesh):
    spec = P(None, "prow", None, None, "pcol", None)
    return jax.shard_map(per_device, mesh=mesh, in_specs=(spec,), out_specs=spec, check_vma=False)
```

```python
import functools

import jax
import jax.numpy as jnp
from jax import lax
from jax.experimental import pallas as pl
from jax.experimental.pallas import tpu as pltpu
from jax.sharding import PartitionSpec as P

MESH = pl.DeviceIdType.MESH
HI = lax.Precision.HIGHEST
NB, PB, MB = 256, 64, 8
T = 5
ROWS = 64
PER = NB // ROWS
SL = 16


def micro(w_ref, r0, pend):
    lane = lax.broadcasted_iota(jnp.int32, (MB, NB), 1)
    sub = lax.broadcasted_iota(jnp.int32, (MB, NB), 0)
    sub1 = lax.broadcasted_iota(jnp.int32, (MB, 128), 0)
    own = (lane >= r0) & (lane < r0 + MB)
    blk = w_ref[r0:r0 + MB, :]
    d = blk[:, r0:r0 + MB]
    rep = {(i, j): jnp.broadcast_to(d[i:i + 1, j:j + 1], (MB, 128)) for i in range(MB) for j in range(i + 1)}
    low, inv = {}, {}
    a = dict(rep)
    rs = []
    for j in range(MB):
        r = lax.rsqrt(a[j, j])
        rs.append(r)
        for i in range(j + 1, MB):
            low[i, j] = a[i, j] * r
        for k in range(j + 1, MB):
            for i in range(k, MB):
                a[i, k] = a[i, k] - low[i, j] * low[k, j]
    for j in range(MB):
        inv[j, j] = rs[j]
        for i in range(j + 1, MB):
            t = low[i, j] * inv[j, j]
            for k in range(j + 1, i):
                t = t + low[i, k] * inv[k, j]
            inv[i, j] = -t * rs[i]
    ainv = {}
    for i in range(MB):
        for j in range(i + 1):
            t = inv[i, i] * inv[i, j]
            for k in range(i + 1, MB):
                t = t + inv[k, i] * inv[k, j]
            ainv[i, j] = ainv[j, i] = t
    aug = []
    for j in range(MB):
        row = jnp.broadcast_to(w_ref[r0 + j:r0 + j + 1, :], (MB, NB))
        aug.append(jnp.where(own, jnp.where(lane == r0 + j, 1.0, 0.0), row))
    def mix(coef, lower):
        out = None
        for j in range(MB):
            col = jnp.zeros((MB, 128), jnp.float32)
            for i in range(j if lower else 0, MB):
                col = jnp.where(sub1 == i, coef[i, j], col)
            term = jnp.concatenate([col, col], axis=1) * aug[j]
            out = term if out is None else out + term
        return out
    z = mix(ainv, False)
    if pend > r0 + MB:
        rows = w_ref[r0 + MB:pend, :]
        n = pend - r0 - MB
        lane_n = lax.broadcasted_iota(jnp.int32, (n, NB), 1)
        acc = jnp.where((lane_n >= r0) & (lane_n < r0 + MB), 0.0, rows)
        for j in range(MB):
            acc = acc - rows[:, r0 + j:r0 + j + 1] * z[j:j + 1, :]
        w_ref[r0 + MB:pend, :] = acc
    w_ref[r0:r0 + MB, :] = mix(inv, True)

def panel(w_ref, kb):
    p0 = kb * PB
    for m in range(PB // MB):
        micro(w_ref, p0 + m * MB, p0 + PB)
    if p0 + PB < NB:
        r = w_ref[p0:p0 + PB, :]
        n = NB - p0 - PB
        lane_r = lax.broadcasted_iota(jnp.int32, (PB, NB), 1)
        sub_r = lax.broadcasted_iota(jnp.int32, (PB, NB), 0) + p0
        solved = jnp.where((lane_r > sub_r) & (lane_r < p0 + PB), 0.0, r)
        rest = w_ref[p0 + PB:NB, :]
        lane_n = lax.broadcasted_iota(jnp.int32, (n, NB), 1)
        rest = jnp.where((lane_n >= p0) & (lane_n < p0 + PB), 0.0, rest)
        up = lax.dot_general(r[:, p0 + PB:NB], solved, (((0,), (0,)), ((), ())), precision=HI, preferred_element_type=jnp.float32)
        w_ref[p0 + PB:NB, :] = rest - up

def inv_rows(w_ref, kb):
    p0 = kb * PB
    x = w_ref[p0:p0 + PB, :]
    lane = lax.broadcasted_iota(jnp.int32, (PB, NB), 1)
    sub = lax.broadcasted_iota(jnp.int32, (PB, NB), 0) + p0
    return jnp.where(lane <= sub, x, 0.0)


ORDER = (1, 2, 3, 4, 0)
STEPS = (("r", 0), ("s", 0), ("r", 1), ("s", 1), ("y", 0), ("r", 2), ("s", 2), ("y", 1), ("r", 3), ("s", 3), ("y", 2), ("r", 4), ("s", 4), ("y", 3), ("y", 4), ("i", 0), ("i", 1), ("i", 2), ("i", 3))


def gather_kernel(a_ref, r_ref, c_ref, i_ref, a_v, w_ref, inv_v, load_sem, send_sem, ysend_sem, csend_sem, r_sem, i_sem, s_sem, x_sem, g_sem):
    p, q = lax.axis_index("prow"), lax.axis_index("pcol")
    x, y, z, c = lax.rem(p, 4), p // 4, q // 2, lax.rem(q, 2)
    both = jnp.logical_and
    source = q == 0
    owner = both(p == 0, source)
    plain_source = both(p != 0, source)
    lead = p == q
    first, second = c == 0, c == 1
    spread = both(q == 1, both(y == 0, x != 0))
    beside_owner = both(q == 1, p == 0)
    bar = pltpu.get_barrier_semaphore()

    def greet(row, col):
        pl.semaphore_signal(bar, 1, device_id=(row, col), device_id_type=MESH)

    def remote(ref, send, recv, row, col):
        return pltpu.make_async_remote_copy(src_ref=ref, dst_ref=ref, send_sem=send, recv_sem=recv, device_id=(row, col), device_id_type=MESH)

    def wait(ref, sem):
        pltpu.make_async_copy(ref, ref, sem).wait()

    def r_chunk(n):
        return r_ref.at[n // PER, pl.ds((n % PER) * ROWS, ROWS), :]

    def i_chunk(m):
        return i_ref.at[pl.ds(m * ROWS, ROWS), :]

    for d in range(1, 4):
        greet(4 * y + lax.rem(x + d, 4), q)
        greet(4 * lax.rem(y + d, 4) + x, q)

    @pl.when(jnp.logical_not(lead))
    def _():
        greet(q, q)

    for kid, parents in ((1, (2,)), (2, (0,)), (3, (2,)), (4, (3, 5)), (5, (6,)), (6, (0,)), (7, (6,))):
        @pl.when(z == kid)
        def _(parents=parents):
            for parent in parents:
                greet(p, 2 * parent + c)

    @pl.when(second)
    def _():
        greet(p, q - 1)

    @pl.when(both(first, jnp.logical_not(owner)))
    def _():
        greet(p, q + 1)

    @pl.when(q == 1)
    def _():
        @pl.when(both(x != 0, y != 0))
        def _():
            greet(x, 1)

        @pl.when(jnp.logical_or(x == 0, y == 0))
        def _():
            greet(0, 0)

    one = lambda cond: jnp.where(cond, 1, 0)
    along = 2 * (one(z == 0) + one(z == 2) + one(z == 6)) + one(z == 3) + one(z == 5)
    expect = 6 + 15 * one(lead) + along + 1 - one(beside_owner) + 3 * one(spread) + 7 * one(owner)

    def greeted():
        pl.semaphore_wait(bar, expect)

    def pass_z(ref, sem, n):
        for parent, kids in ((0, (2, 6)), (2, (1, 3)), (6, (5, 7)), (3 if n % 2 == 0 else 5, (4,))):
            @pl.when(z == parent)
            def _(kids=kids):
                for slot, kid in enumerate(kids):
                    remote(ref, send_sem.at[slot], sem, p, 2 * kid + c).start()

    def send_r(t):
        for n in range(PER * t, PER * t + PER):
            pass_z(r_chunk(n), r_sem.at[n], n)
            remote(r_chunk(n), send_sem.at[2], r_sem.at[n], p, q + 1).start()

    def relay_i(m):
        wait(i_chunk(m), i_sem.at[m])

        @pl.when(spread)
        def _():
            for k in range(1, 4):
                remote(i_chunk(m), ysend_sem.at[k - 1], i_sem.at[m], 4 * k + x, 1).start()
        pass_z(i_chunk(m), i_sem.at[m], m)

        @pl.when(jnp.logical_not(beside_owner))
        def _():
            remote(i_chunk(m), send_sem.at[2], i_sem.at[m], p, q - 1).start()

    mine = pl.ds(pl.multiple_of(p * SL, SL), SL)

    def scatter_part(t, j):
        for i in range(PER):
            row = PER * j + i
            part = pl.ds(row * SL, SL)

            @pl.when(p != row)
            def _(row=row, part=part):
                pltpu.make_async_remote_copy(
                    src_ref=r_ref.at[t, part, :], dst_ref=c_ref.at[t, part, :], send_sem=csend_sem.at[0],
                    recv_sem=s_sem.at[t], device_id=(row, q), device_id_type=MESH).start()

            @pl.when(p == row)
            def _(part=part):
                pltpu.make_async_copy(r_ref.at[t, part, :], c_ref.at[t, part, :], s_sem.at[t]).start()

    def scatter(t):
        for j in range(PER):
            scatter_part(t, j)

    def share(t):
        wait(c_ref.at[t, mine, :], s_sem.at[t])
        for d in range(1, 4):
            remote(c_ref.at[t, mine, :], csend_sem.at[1], x_sem.at[t], 4 * y + lax.rem(x + d, 4), q).start()

    def share_y(t):
        wait(c_ref.at[t, pl.ds(0, 3 * SL), :], x_sem.at[t])
        ours = c_ref.at[t, pl.ds(pl.multiple_of(y * 4 * SL, 4 * SL), 4 * SL), :]
        for d in range(1, 4):
            remote(ours, csend_sem.at[2], g_sem.at[t], 4 * lax.rem(y + d, 4) + x, q).start()

    def load(t):
        return pltpu.make_async_copy(a_ref.at[t, 0, :, 0, 0, :], r_ref.at[t], load_sem.at[t])

    def factor(kb):
        panel(w_ref, kb)
        inv_v[kb * PB:(kb + 1) * PB, :] = inv_rows(w_ref, kb)

    def give(m):
        src = inv_v.at[pl.ds(m * ROWS, ROWS), :]
        for slot, row in enumerate((1, 2, 3, 4, 8, 12, 0)):
            pltpu.make_async_remote_copy(src_ref=src, dst_ref=i_chunk(m), send_sem=ysend_sem.at[slot], recv_sem=i_sem.at[m], device_id=(row, 1), device_id_type=MESH).start()
        pltpu.make_async_copy(src, i_chunk(m), i_sem.at[m]).start()

    @pl.when(owner)
    def _():
        lead_tile = pltpu.make_async_copy(a_ref.at[0, 0, :, 0, 0, :], a_v, load_sem.at[0])
        lead_tile.start()
        for t in range(1, T):
            load(t).start()
        lead_tile.wait()
        a = a_v[...]
        w_ref[...] = 0.5 * (a + a.T)
        a_v[...] = w_ref[...]
        kept = pltpu.make_async_copy(a_v, r_ref.at[0], load_sem.at[0])
        kept.start()
        factor(0)
        factor(1)
        kept.wait()
        for t in range(1, T):
            load(t).wait()
        greeted()
        give(0)
        give(1)
        for t in (1, 2):
            send_r(t)
            scatter(t)
        factor(2)
        give(2)
        send_r(3)
        scatter(3)
        factor(3)
        give(3)
        for t in (4, 0):
            send_r(t)
            scatter(t)

    @pl.when(plain_source)
    def _():
        for t in ORDER:
            load(t).start()
        greeted()
        for t in ORDER:
            load(t).wait()
            send_r(t)

    @pl.when(source)
    def _():
        for n, t in enumerate(ORDER):
            share(t)
            if n > 0:
                share_y(ORDER[n - 1])
        share_y(ORDER[-1])

    @pl.when(q != 0)
    def _():
        greeted()

    def take(t):
        for n in range(PER * t, PER * t + PER):
            wait(r_chunk(n), r_sem.at[n])

            @pl.when(first)
            def _(n=n):
                pass_z(r_chunk(n), r_sem.at[n], n)
                remote(r_chunk(n), send_sem.at[2], r_sem.at[n], p, q + 1).start()

            @pl.when(lead)
            def _(n=n):
                scatter_part(t, n % PER)

    @pl.when(q != 0)
    def _():
        for step in STEPS:
            kind, n = step
            if kind == "r":
                take(ORDER[n])
            elif kind == "s":
                share(ORDER[n])
            elif kind == "y":
                share_y(ORDER[n])
            else:
                pl.when(second)(functools.partial(relay_i, n))

    @pl.when(first)
    def _():
        for m in range(4):
            wait(i_chunk(m), i_sem.at[m])
    for t in ORDER:
        wait(c_ref.at[t, pl.ds(0, NB - 4 * SL), :], g_sem.at[t])
    wait(c_ref.at[:, pl.ds(0, 3 * SL), :], csend_sem.at[1])
    wait(c_ref.at[:, pl.ds(0, NB - 4 * SL), :], csend_sem.at[2])

    @pl.when(lead)
    def _():
        wait(c_ref.at[:, pl.ds(0, NB - SL), :], csend_sem.at[0])

    @pl.when(owner)
    def _():
        for k in range(7):
            wait(i_ref, ysend_sem.at[k])

    @pl.when(spread)
    def _():
        for k in range(3):
            wait(i_ref, ysend_sem.at[k])

    wide = jnp.logical_or(z == 0, jnp.logical_or(z == 2, z == 6))
    half = jnp.logical_or(z == 3, z == 5)

    @pl.when(first)
    def _():
        wait(r_ref, send_sem.at[2])

        @pl.when(wide)
        def _():
            wait(r_ref, send_sem.at[0])
            wait(r_ref, send_sem.at[1])

        @pl.when(half)
        def _():
            wait(r_ref.at[:, pl.ds(0, NB // 2), :], send_sem.at[0])

    @pl.when(second)
    def _():
        @pl.when(jnp.logical_not(beside_owner))
        def _():
            wait(i_ref, send_sem.at[2])

        @pl.when(wide)
        def _():
            wait(i_ref, send_sem.at[0])
            wait(i_ref, send_sem.at[1])

        @pl.when(half)
        def _():
            wait(i_ref.at[pl.ds(0, NB // 2), :], send_sem.at[0])


def gather(matrix):
    tiles = jax.ShapeDtypeStruct((T, NB, NB), jnp.float32)
    square = jax.ShapeDtypeStruct((NB, NB), jnp.float32)
    dma = pltpu.SemaphoreType.DMA
    return pl.pallas_call(
        gather_kernel,
        out_shape=(tiles, tiles, square),
        in_specs=[pl.BlockSpec(memory_space=pltpu.HBM)],
        out_specs=[pl.BlockSpec(memory_space=pl.ANY)] * 3,
        scratch_shapes=[
            pltpu.VMEM((NB, NB), jnp.float32), pltpu.VMEM((NB, NB), jnp.float32), pltpu.VMEM((NB, NB), jnp.float32),
            dma((T,)), dma((3,)), dma((7,)), dma((3,)), dma((T * PER,)), dma((4,)), dma((T,)), dma((T,)), dma((T,)),
        ],
        compiler_params=pltpu.CompilerParams(collective_id=0, has_side_effects=True, vmem_limit_bytes=50 * 2**20),
        name="gather",
    )(matrix)


def split(v):
    high = v.astype(jnp.bfloat16)
    return high, (v - high.astype(jnp.float32)).astype(jnp.bfloat16)


def left_parts(v):
    high, low = split(v)
    return jnp.concatenate([high, high, low], axis=1)


def right_parts(v):
    high, low = split(v)
    return jnp.concatenate([high, low, high], axis=1)


def times(left, right):
    return lax.dot_general(left, right, (((1,), (1,)), ((), ())), preferred_element_type=jnp.float32)


LANES = 128
STRIDE = T * NB // LANES
ROW_LINES = NB * STRIDE


def update_kernel(a_ref, r_ref, c_ref, i_ref, o_ref, o_v, x_v, inv3, r3, c3, store_sem):
    p, q = lax.axis_index("prow"), lax.axis_index("pcol")

    def lines(k, j, h):
        return pl.ds(k * ROW_LINES + j * (NB // LANES) + h, NB, stride=STRIDE)

    def put(k, j, v):
        for h in range(NB // LANES):
            o_v[lines(k, j, h), :] = v[:, h * LANES:(h + 1) * LANES]

    def store(k):
        part = pl.ds(k * ROW_LINES, ROW_LINES)
        return pltpu.make_async_copy(o_v.at[part, :], o_ref.at[part, :], store_sem.at[k])

    inv3[...] = right_parts(i_ref[...])
    for k in range(T):
        c3[k] = right_parts(times(left_parts(c_ref[k]), inv3[...]))
    for k in range(T):
        v = times(left_parts(r_ref[k]), inv3[...])
        r3[k] = left_parts(v)
        x_v[...] = v
        if k == 0:
            @pl.when(jnp.logical_and(p == 0, q == 0))
            def _():
                row = lax.broadcasted_iota(jnp.int32, (NB, NB), 0)
                col = lax.broadcasted_iota(jnp.int32, (NB, NB), 1)
                x_v[...] = jnp.where(col <= row, x_v[...], 0.0)
        for j in range(T):
            if j > k:
                put(k, j, jnp.zeros((NB, NB), jnp.float32))
                continue
            a = jnp.concatenate([a_ref[lines(k, j, h), :] for h in range(NB // LANES)], axis=1)
            v = a - times(r3[k], c3[j])
            if k == j:
                v = jnp.where(p >= q, v, 0.0)
            if j == 0:
                v = jnp.where(q == 0, x_v[...], v)
            put(k, j, v)
        store(k).start()
    for k in range(T):
        store(k).wait()


def update(matrix, r, c, i):
    vmem = pl.BlockSpec(memory_space=pltpu.VMEM)
    flat = (matrix.size // LANES, LANES)
    thirds = pltpu.VMEM((T, NB, 3 * NB), jnp.bfloat16)
    out = pl.pallas_call(
        update_kernel,
        out_shape=jax.ShapeDtypeStruct(flat, jnp.float32),
        in_specs=[vmem, vmem, vmem, vmem],
        out_specs=pl.BlockSpec(memory_space=pl.ANY),
        scratch_shapes=[
            pltpu.VMEM(flat, jnp.float32), pltpu.VMEM((NB, NB), jnp.float32), pltpu.VMEM((NB, 3 * NB), jnp.bfloat16), thirds, thirds,
            pltpu.SemaphoreType.DMA((T,)),
        ],
        compiler_params=pltpu.CompilerParams(vmem_limit_bytes=32 * 2**20),
        name="update",
    )(matrix.reshape(flat), r, c, i)
    return out.reshape(matrix.shape)


def per_device(matrix):
    r, c, i = gather(matrix)
    return update(matrix, r, c, i)


def solution(mesh):
    spec = P(None, "prow", None, None, "pcol", None)
    return jax.shard_map(per_device, mesh=mesh, in_specs=(spec,), out_specs=spec, check_vma=False)
```
